32 devices in a mesh: shard: 2 (over y), rep: 16 (over z, x, core).
Axes of the slice: x: 2, y: 2, z: 4, core: 2. Of those that a mesh axis runs over, the one named last changes fastest.
Arguments:
- tokens: bfloat16 [32768, 768], P(('shard', 'rep')), may hold values from -6 to 6
- lengths: int32 [32], P(('shard', 'rep')), may hold values from 513 to 1024, as said below
- cotangent: bfloat16 [32768, 768], P(('shard', 'rep')), may hold values from -6 to 6
- gain_one: bfloat16 [768], P('shard'), may hold values from 0.25 to 1.75
- shift_one: bfloat16 [768], P('shard'), may hold values from -3 to 3
- attend_weight: bfloat16 [768, 2304], P('shard'), may hold values from -0.375 to 0.375
- attend_bias: bfloat16 [1536], P('shard'), may hold values from -0.29882812 to 0.29882812
- mixing_weight: bfloat16 [768, 768], P('shard'), may hold values from -0.21875 to 0.21875
- mixing_bias: bfloat16 [768], P('shard'), may hold values from -3 to 3
- gain_two: bfloat16 [768], P('shard'), may hold values from 0.25 to 1.75
- shift_two: bfloat16 [768], P('shard'), may hold values from -3 to 3
- expand_weight: bfloat16 [768, 3072], P('shard'), may hold values from -0.21875 to 0.21875
- expand_bias: bfloat16 [3072], P('shard'), may hold values from -3 to 3
- reduce_weight: bfloat16 [3072, 768], P('shard'), may hold values from -0.109375 to 0.109375
- reduce_bias: bfloat16 [768], P('shard'), may hold values from -3 to 3
Outputs:
- block_output: bfloat16 [32768, 768], P(('shard', 'rep'))
- tokens_slope: bfloat16 [32768, 768], P(('shard', 'rep'))
- gain_one_slope: float32 [768], P('shard')
- shift_one_slope: float32 [768], P('shard')
- attend_weight_slope: float32 [768, 2304], P('shard')
- attend_bias_slope: float32 [1536], P('shard')
- mixing_weight_slope: float32 [768, 768], P('shard')
- mixing_bias_slope: float32 [768], P('shard')
- gain_two_slope: float32 [768], P('shard')
- shift_two_slope: float32 [768], P('shard')
- expand_weight_slope: float32 [768, 3072], P('shard')
- expand_bias_slope: float32 [3072], P('shard')
- reduce_weight_slope: float32 [3072, 768], P('shard')
- reduce_bias_slope: float32 [768], P('shard')
The draws below stay inside these ranges and needn't reach their ends.
Inputs may be any that keep to these rules, and one draw needn't show every extreme that they name: `lengths`: each sequence's real tokens fill the front of its 1024 slots, more than half of them; the rest are padding.
All inputs are finite; a program needn't handle non-finite values.
Results may differ from the reference program's by a relative error of at most 0.02.
Values may be sent and summed in bfloat16 or wider, within the bound.
A program may use at most 256 MiB of HBM per device.

```python
import jax
import jax.numpy as jnp
from jax import lax

D = 768
H = 12
HD = 64
FF = 3072
SEQ = 1024
NSEQ = 32
TOKENS = 32768


def draw_lengths(key, part):
    counts = jax.random.randint(key, (NSEQ,), SEQ // 2 + 1, SEQ + 1)
    return counts.at[0].set(SEQ).astype(jnp.int32)


def level_of(rng, extent, cuts, low, top_value):
    factor_of, own = 1.0, jax.random.fold_in(rng, 6)
    for axis_at, parts in cuts:
        steps = jnp.exp(jax.random.uniform(jax.random.fold_in(own, axis_at), (parts,), jnp.float32, low / len(cuts), top_value / len(cuts)))
        factor_of = factor_of * jnp.repeat(steps, extent[axis_at] // parts).reshape([-1 if axis == axis_at else 1 for axis in range(len(extent))])
    return factor_of


def noise(stream_key, dims, deviation, bound, shards=(), held_as=jnp.bfloat16):
    loudness = level_of(stream_key, dims, shards, -0.22, 0.18) if shards else 1.0
    array = jax.random.normal(stream_key, dims, jnp.float32) * deviation * loudness
    return jnp.minimum(jnp.maximum(array, -bound), bound).astype(held_as)


def setup_inputs(seed: int = 0) -> dict:
    arg_keys = jax.random.split(jax.random.key(seed), 16)
    tokens = noise(arg_keys[0], (TOKENS, D), 1.0, 6.0, ((0, 32),))
    lengths = draw_lengths(jax.random.fold_in(arg_keys[15], 71), 0)
    cotangent = noise(arg_keys[2], (TOKENS, D), 1.0, 6.0, ((0, 32),))
    gain_one = jnp.clip(1.0 + 0.15 * jax.random.normal(arg_keys[3], (D,), jnp.float32), 0.25, 1.75).astype(jnp.bfloat16)
    shift_one = noise(arg_keys[4], (D,), 0.3, 3.0, ((0, 2),))
    attend_weight = noise(arg_keys[5], (D, 3 * D), (D // 3) ** -0.5, 0.375, ((0, 2),))
    attend_bias = noise(arg_keys[6], (2 * D,), 0.03, 0.29882812, ((0, 2),))
    mixing_weight = noise(arg_keys[7], (D, D), D ** -0.5, 0.21875, ((0, 2),))
    mixing_bias = noise(arg_keys[8], (D,), 0.3, 3.0, ((0, 2),))
    gain_two = jnp.clip(1.0 + 0.15 * jax.random.normal(arg_keys[9], (D,), jnp.float32), 0.25, 1.75).astype(jnp.bfloat16)
    shift_two = noise(arg_keys[10], (D,), 0.3, 3.0, ((0, 2),))
    expand_weight = noise(arg_keys[11], (D, FF), D ** -0.5, 0.21875, ((0, 2),))
    expand_bias = noise(arg_keys[12], (FF,), 0.3, 3.0, ((0, 2),))
    reduce_weight = noise(arg_keys[13], (FF, D), FF ** -0.5, 0.109375, ((0, 2),))
    reduce_bias = noise(arg_keys[14], (D,), 0.3, 3.0, ((0, 2),))
    return dict(tokens=tokens, lengths=lengths, cotangent=cotangent, gain_one=gain_one, shift_one=shift_one, attend_weight=attend_weight, attend_bias=attend_bias, mixing_weight=mixing_weight, mixing_bias=mixing_bias, gain_two=gain_two, shift_two=shift_two, expand_weight=expand_weight, expand_bias=expand_bias, reduce_weight=reduce_weight, reduce_bias=reduce_bias)


@jax.custom_vjp
def low(v):
    return lax.optimization_barrier(v.astype(jnp.bfloat16)).astype(jnp.float32)

@jax.custom_vjp
def low_back(v):
    return v

def low_keep(v):
    return (low(v), None)

def low_pass(kept, grad):
    return (grad,)

def back_keep(v):
    return (v, None)

def back_low(kept, grad):
    return (low(grad),)
low.defvjp(low_keep, low_pass)
low_back.defvjp(back_keep, back_low)

def matmul(left, right):
    return jnp.dot(left, right, precision=lax.Precision.HIGHEST)

def normalize(values, gain, shift):
    center = values - lax.optimization_barrier(jnp.mean(values, axis=-1, keepdims=True))
    spread = lax.rsqrt(lax.optimization_barrier(jnp.mean(center * center, axis=-1, keepdims=True)) + 1e-05)
    return center * spread * gain + shift

def attention(query, keys, values, length):
    block = min(512, SEQ)
    count = SEQ // block
    scale = 1.0 / HD ** 0.5
    keyvalid = lax.iota(jnp.int32, SEQ) < length

    def one_block(piece):
        scores = jnp.einsum('qhd,khd->hqk', piece, keys, precision=lax.Precision.HIGHEST) * scale
        scores = jnp.where(keyvalid[None, None, :], scores, -1e+30)
        scores = low_back(scores)
        probs = low(jax.nn.softmax(scores, axis=-1))
        return jnp.einsum('hqk,khd->qhd', probs, values, precision=lax.Precision.HIGHEST)
    pieces = query.reshape(count, block, H, HD)
    mixed = lax.map(jax.checkpoint(one_block), pieces)
    return mixed.reshape(SEQ, D)

def block_forward(rows, length, params):
    gain_one, shift_one, attend_weight, attend_bias, mixing_weight, mixing_bias, gain_two, shift_two, expand_weight, expand_bias, reduce_weight, reduce_bias = params
    live = (lax.iota(jnp.int32, SEQ) < length).astype(rows.dtype)[:, None]
    first = low(normalize(rows, gain_one, shift_one))
    zeros = jnp.zeros((D,), rows.dtype)
    full_bias = jnp.concatenate([attend_bias[:D], zeros, attend_bias[D:]])
    mixed = matmul(first, low(attend_weight)) + full_bias
    query = low(low_back(mixed[:, :D])).reshape(SEQ, H, HD)
    keys = low(low_back(mixed[:, D:2 * D])).reshape(SEQ, H, HD)
    values = low(low_back(mixed[:, 2 * D:])).reshape(SEQ, H, HD)
    attended = low(low_back(attention(query, keys, values, length)))
    branch = low_back(matmul(attended, low(mixing_weight)) + mixing_bias)
    middle = rows + branch
    second = low(normalize(middle, gain_two, shift_two))
    hidden = low_back(matmul(second, low(expand_weight)) + expand_bias)
    active = low(hidden * jax.nn.sigmoid(1.702 * hidden))
    final = low_back(matmul(active, low(reduce_weight)) + reduce_bias)
    return live * (middle + final)

def reference(tokens, lengths, cotangent, gain_one, shift_one, attend_weight, attend_bias, mixing_weight, mixing_bias, gain_two, shift_two, expand_weight, expand_bias, reduce_weight, reduce_bias):
    params = tuple((item.astype(jnp.float32) for item in (gain_one, shift_one, attend_weight, attend_bias, mixing_weight, mixing_bias, gain_two, shift_two, expand_weight, expand_bias, reduce_weight, reduce_bias)))
    rows_all = tokens.astype(jnp.float32).reshape(NSEQ, SEQ, D)
    upstream_all = cotangent.astype(jnp.float32).reshape(NSEQ, SEQ, D)

    def step(totals, item):
        rows, length, upstream = item
        result, pullback = jax.vjp(lambda inner, weights: block_forward(inner, length, weights), rows, params)
        d_rows, d_params = pullback(upstream)
        totals = jax.tree.map(lambda acc, term: acc + term, totals, d_params)
        return (totals, (result.astype(jnp.bfloat16), d_rows.astype(jnp.bfloat16)))
    initial = tuple((jnp.zeros_like(item) for item in params))
    totals, (outputs, slopes) = lax.scan(step, initial, (rows_all, lengths.astype(jnp.int32), upstream_all))
    return (outputs.reshape(TOKENS, D), slopes.reshape(TOKENS, D), totals[0], totals[1], totals[2], totals[3], totals[4], totals[5], totals[6], totals[7], totals[8], totals[9], totals[10], totals[11])
```

```python
import functools

import jax
import jax.numpy as jnp
from jax import lax
from jax.experimental import pallas as pl
from jax.experimental.pallas import tpu as pltpu
from jax.sharding import PartitionSpec as P

D = 768
H = 12
SEQ = 1024
FF = 3072
bf = jnp.bfloat16
f32 = jnp.float32
NN = (((1,), (0,)), ((), ()))
NT = (((1,), (1,)), ((), ()))
TN = (((0,), (0,)), ((), ()))
VM = pl.BlockSpec(memory_space=pltpu.VMEM)
SM = pl.BlockSpec(memory_space=pltpu.SMEM)
HB = pl.BlockSpec(memory_space=pl.ANY)
VLIMIT = 60 * 2**20
RB = 256


def dot(a, b, dims=NN):
    return lax.dot_general(a, b, dims, preferred_element_type=f32)


def lanes(shape):
    return lax.broadcasted_iota(jnp.int32, shape, 1)


def rowsi(shape):
    return lax.broadcasted_iota(jnp.int32, shape, 0)


def norm(v):
    mean = jnp.mean(v, axis=-1, keepdims=True)
    c = v - mean
    r = lax.rsqrt(jnp.mean(c * c, axis=-1, keepdims=True) + 1e-05)
    return c * r, r


def norm_back(up, n, r, gain):
    e = up * gain
    return r * (e - jnp.mean(e, axis=-1, keepdims=True) - n * jnp.mean(e * n, axis=-1, keepdims=True))


def three(v):
    hi = v.astype(bf).astype(f32)
    mid = (v - hi).astype(bf).astype(f32)
    return hi, mid, v - hi - mid


def fwd_pair(hp, length, qkv_ref, o_ref, lse_ref):
    QB = 512
    cq = pl.multiple_of(hp * 128, 128)
    q = qkv_ref[:, pl.ds(cq, 128)]
    k = qkv_ref[:, pl.ds(pl.multiple_of(cq + D, 128), 128)]
    v = qkv_ref[:, pl.ds(pl.multiple_of(cq + 2 * D, 128), 128)]
    vt = v.T
    ln = lanes((SEQ, 128))
    rw = rowsi((SEQ, 128))
    kaug = jnp.where((ln == 0) & (rw >= length), -1e30, 0.0).astype(bf)
    qaug = (lanes((QB, 128)) == 0).astype(f32).astype(bf)
    vr = rowsi((128, SEQ))
    ksides = []
    vts = []
    for h in range(2):
        half = (ln < 64) if h == 0 else (ln >= 64)
        ksides.append(jnp.concatenate([jnp.where(half, k, jnp.zeros_like(k)), kaug], axis=1))
        vh = (vr < 64) if h == 0 else (vr >= 64)
        vts.append(jnp.where(vh, vt, jnp.ones_like(vt)))
    items = [(qb, h) for qb in range(SEQ // QB) for h in range(2)]

    def scores(it):
        qb, h = it
        qs = jnp.concatenate([q[qb * QB : (qb + 1) * QB], qaug], axis=1)
        return dot(ksides[h], qs, NT)

    res = {}
    s_next = scores(items[0])
    for i, it in enumerate(items):
        s = s_next
        if i + 1 < len(items):
            s_next = scores(items[i + 1])
        m = jnp.max(s, axis=0, keepdims=True)
        p = jnp.exp(s - m).astype(bf)
        ot = dot(vts[it[1]], p)
        qb, h = it
        total = ot[64:65] if h == 0 else ot[0:1]
        res[it] = ot / total
        lse_ref[pl.ds(2 * hp + h, 1), qb * QB : (qb + 1) * QB] = m + jnp.log(total)
        if h == 1:
            op = jnp.where(rowsi((128, QB)) < 64, res[(qb, 0)], res[(qb, 1)])
            o_ref[qb * QB : (qb + 1) * QB, pl.ds(cq, 128)] = op.astype(bf).T


def bwd_pair(hp, length, qkv_ref, do_ref, augq_ref, augd_ref, dqkv_ref):
    KB = 512
    cq = pl.multiple_of(hp * 128, 128)
    ck = pl.multiple_of(cq + D, 128)
    cv = pl.multiple_of(cq + 2 * D, 128)
    q = qkv_ref[:, pl.ds(cq, 128)]
    k = qkv_ref[:, pl.ds(ck, 128)]
    v = qkv_ref[:, pl.ds(cv, 128)]
    do = do_ref[:, pl.ds(cq, 128)]
    qt = q.T
    dot_ = do.T
    qs = jnp.concatenate([q, augq_ref[...]], axis=1)
    ds_ = jnp.concatenate([do, augd_ref[...]], axis=1)
    lb = lanes((KB, 128))
    rb = rowsi((KB, 128))

    def first(it):
        kb, h = it
        half = (lb < 64) if h == 0 else (lb >= 64)
        hh = 2 * hp + h
        neg = jnp.where((lb == hh) | (lb == hh + 16) | (lb == hh + 32), -1.0, 0.0)
        aug = jnp.where((lb == 48) & (rb + kb * KB >= length), -1e30, neg).astype(bf)
        kk = k[kb * KB : (kb + 1) * KB]
        vv = v[kb * KB : (kb + 1) * KB]
        z = jnp.zeros_like(kk)
        ks = jnp.concatenate([jnp.where(half, kk, z), aug], axis=1)
        vs = jnp.concatenate([jnp.where(half, vv, z), aug], axis=1)
        return dot(qs, ks, NT), dot(ds_, vs, NT), kk

    items = [(kb, h) for kb in range(SEQ // KB) for h in range(2)]
    dq = [None, None]
    dk = {}
    dv = {}
    nxt = first(items[0])
    for i, it in enumerate(items):
        s, dp, kk = nxt
        if i + 1 < len(items):
            nxt = first(items[i + 1])
        kb, h = it
        p = jnp.exp(s)
        pb = p.astype(bf)
        dsb = (p * dp).astype(bf)
        rs = slice(0, 64) if h == 0 else slice(64, 128)
        dv[it] = dot(dot_[rs], pb)
        dk[it] = dot(qt[rs], dsb)
        t = dot(dsb, kk)
        dq[h] = t if dq[h] is None else dq[h] + t
        if h == 1:
            dkp = jnp.concatenate([dk[(kb, 0)], dk[(kb, 1)]], axis=0).astype(bf)
            dvp = jnp.concatenate([dv[(kb, 0)], dv[(kb, 1)]], axis=0).astype(bf)
            dqkv_ref[kb * KB : (kb + 1) * KB, pl.ds(ck, 128)] = dkp.T
            dqkv_ref[kb * KB : (kb + 1) * KB, pl.ds(cv, 128)] = dvp.T
    dqkv_ref[:, pl.ds(cq, 128)] = (jnp.where(lanes((SEQ, 128)) < 64, dq[0], dq[1]) * 0.125).astype(bf)


def front_kernel(len_ref, x_ref, g_ref, b_ref, wa_ref, ba_ref, h_ref, qkv_ref, o_ref, aug_ref, lse_ref):
    length = len_ref[0]

    def rows(i, _):
        r = pl.ds(pl.multiple_of(i * RB, RB), RB)
        n, _r = norm(x_ref[r, :].astype(f32))
        h_ref[r, :] = (n * g_ref[...] + b_ref[...]).astype(bf)
        return 0

    lax.fori_loop(0, SEQ // RB, rows, 0)

    def cols(j, _):
        c = pl.ds(pl.multiple_of(j * 256, 256), 256)
        t = dot(h_ref[...], wa_ref[:, c]) + ba_ref[:, c]
        t = t.astype(bf).astype(f32) * jnp.where(j < D // 256, 0.125, 1.0)
        qkv_ref[:, c] = t.astype(bf)
        return 0

    lax.fori_loop(0, 3 * D // 256, cols, 0)
    lse_ref[...] = jnp.zeros_like(lse_ref)

    def pair(hp, _):
        fwd_pair(hp, length, qkv_ref, o_ref, lse_ref)
        return 0

    lax.fori_loop(0, H // 2, pair, 0)
    hi, mid, lo = three(lse_ref[...])
    one = jnp.where(rowsi((80, SEQ)) == 0, 1.0, 0.0)
    aug_ref[...] = jnp.concatenate([hi, mid, lo, one], axis=0).astype(bf).T


def front(length, x, g1, b1, wa, ba):
    return pl.pallas_call(
        front_kernel,
        out_shape=(
            jax.ShapeDtypeStruct((SEQ, D), bf),
            jax.ShapeDtypeStruct((SEQ, 3 * D), bf),
            jax.ShapeDtypeStruct((SEQ, D), bf),
            jax.ShapeDtypeStruct((SEQ, 128), bf),
        ),
        in_specs=[SM] + [VM] * 5,
        out_specs=(VM,) * 4,
        scratch_shapes=[pltpu.VMEM((16, SEQ), f32)],
        compiler_params=pltpu.CompilerParams(vmem_limit_bytes=VLIMIT),
        cost_estimate=pl.CostEstimate(flops=7 * 10**9, bytes_accessed=10**7, transcendentals=12 * 2**20),
        name="front",
    )(length, x, g1, b1, wa, ba)


def mid_kernel(
    W, len_ref, x_ref, o_ref, cot_ref, wo_ref, bo_ref, g_ref, b_ref, w1_any, be_ref, w2_any, br_ref,
    out_ref, dx_ref, do_ref, augd_ref, dw1_ref, dw2_ref, dwo_ref, dbe_ref, dsm_ref,
    w1_ref, w2_ref, x1_ref, y_ref, dh_ref, h_ref, gb_ref, dxb_ref, sem,
):
    length = len_ref[0]
    c1 = pltpu.make_async_copy(w1_any, w1_ref, sem.at[0])
    c2 = pltpu.make_async_copy(w2_any, w2_ref, sem.at[1])
    c1.start()
    c2.start()

    def rows(i, acc):
        r = pl.ds(pl.multiple_of(i * RB, RB), RB)
        x1 = x_ref[r, :].astype(f32) + (dot(o_ref[r, :], wo_ref[...]) + bo_ref[...])
        x1_ref[r, :] = x1
        n, _r = norm(x1)
        h_ref[r, :] = (n * g_ref[...] + b_ref[...]).astype(bf)
        live = (rowsi((RB, 1)) + i * RB) < length
        gb = jnp.where(live, cot_ref[r, :].astype(f32), 0.0)
        gb_ref[r, :] = gb.astype(bf)
        y_ref[r, :] = jnp.zeros((RB, D), f32)
        dh_ref[r, :] = jnp.zeros((RB, D), f32)
        return acc + jnp.sum(gb, axis=0, keepdims=True)

    dsm_ref[0:1, :] = lax.fori_loop(0, SEQ // RB, rows, jnp.zeros((1, D), f32))
    c1.wait()
    c2.wait()

    def chunk(j, _):
        lo = pl.multiple_of(j * W, W)
        parts = [pl.ds(pl.multiple_of(lo + s * (FF // 2), W), W) for s in range(2)]
        for s, c in enumerate(parts):
            w1 = w1_ref[:, c]
            w2 = w2_ref[c, :]
            u = dot(h_ref[...], w1) + be_ref[:, c]
            sig = 0.5 * jnp.tanh(0.851 * u) + 0.5
            a = u * sig
            ab = a.astype(bf)
            y_ref[...] += dot(ab, w2)
            dw2_ref[c, :] = dot(ab, gb_ref[...], TN).astype(bf)
            da = dot(gb_ref[...], w2, NT)
            du = da * (sig * (1.0 + 1.702 * (u - a)))
            dub = du.astype(bf)
            dbe_ref[:, c] = jnp.sum(du, axis=0, keepdims=True)
            dw1_ref[:, c] = dot(h_ref[...], dub, TN).astype(bf)
            dh_ref[...] += dot(dub, w1, NT)
        return 0

    lax.fori_loop(0, FF // (2 * W), chunk, 0)
    hl = lanes((D, 128)) % 16
    sel = jnp.where((hl == rowsi((D, 128)) // 64) & (lanes((D, 128)) < 48), 1.0, 0.0).astype(bf)

    def last(i, acc):
        r = pl.ds(pl.multiple_of(i * RB, RB), RB)
        x1 = x1_ref[r, :]
        live = (rowsi((RB, 1)) + i * RB) < length
        out_ref[r, :] = jnp.where(live, x1 + (y_ref[r, :] + br_ref[...]), 0.0).astype(bf)
        n, rs = norm(x1)
        dh = dh_ref[r, :]
        dx = gb_ref[r, :].astype(f32) + norm_back(dh, n, rs, g_ref[...])
        dx_ref[r, :] = dx
        dxb = dx.astype(bf)
        dxb_ref[r, :] = dxb
        do = dot(dxb, wo_ref[...], NT).astype(bf)
        do_ref[r, :] = do
        prod = do.astype(f32) * o_ref[r, :].astype(f32)
        phi = prod.astype(bf)
        dl = dot(phi, sel) + dot((prod - phi.astype(f32)).astype(bf), sel)
        hi, mid, lo = three(dl)
        ln = lanes((RB, 128))
        augd_ref[r, :] = jnp.where(ln < 16, hi, jnp.where(ln < 32, mid, lo)).astype(bf)
        return (
            acc[0] + jnp.sum(dh * n, axis=0, keepdims=True),
            acc[1] + jnp.sum(dh, axis=0, keepdims=True),
            acc[2] + jnp.sum(dx, axis=0, keepdims=True),
        )

    z = jnp.zeros((1, D), f32)
    a0, a1, a2 = lax.fori_loop(0, SEQ // RB, last, (z, z, z))
    dsm_ref[1:2, :] = a0
    dsm_ref[2:3, :] = a1
    dsm_ref[3:4, :] = a2
    dwo_ref[...] = dot(o_ref[...], dxb_ref[...], TN).astype(bf)


def middle(length, x, o, cot, wo, bo, g2, b2, w1, be, w2, br):
    return pl.pallas_call(
        functools.partial(mid_kernel, 256),
        out_shape=(
            jax.ShapeDtypeStruct((SEQ, D), bf),
            jax.ShapeDtypeStruct((SEQ, D), f32),
            jax.ShapeDtypeStruct((SEQ, D), bf),
            jax.ShapeDtypeStruct((SEQ, 128), bf),
            jax.ShapeDtypeStruct((D, FF), bf),
            jax.ShapeDtypeStruct((FF, D), bf),
            jax.ShapeDtypeStruct((D, D), bf),
            jax.ShapeDtypeStruct((1, FF), f32),
            jax.ShapeDtypeStruct((4, D), f32),
        ),
        in_specs=[SM] + [VM] * 7 + [HB, VM, HB, VM],
        out_specs=(VM,) * 9,
        scratch_shapes=[
            pltpu.VMEM((D, FF), bf),
            pltpu.VMEM((FF, D), bf),
            pltpu.VMEM((SEQ, D), f32),
            pltpu.VMEM((SEQ, D), f32),
            pltpu.VMEM((SEQ, D), f32),
            pltpu.VMEM((SEQ, D), bf),
            pltpu.VMEM((SEQ, D), bf),
            pltpu.VMEM((SEQ, D), bf),
            pltpu.SemaphoreType.DMA((2,)),
        ],
        compiler_params=pltpu.CompilerParams(vmem_limit_bytes=VLIMIT),
        cost_estimate=pl.CostEstimate(flops=33 * 10**9, bytes_accessed=3 * 10**7, transcendentals=3 * 2**20),
        name="middle",
    )(length, x, o, cot, wo, bo, g2, b2, w1, be, w2, br)


def back_kernel(len_ref, qkv_ref, do_ref, augq_ref, augd_ref, h_ref, x_ref, dx_ref, g_ref, wa_ref,
                ts_ref, dwa_ref, dba_ref, dsm_ref, dqkv_ref, dh_ref):
    length = len_ref[0]

    def pair(hp, _):
        bwd_pair(hp, length, qkv_ref, do_ref, augq_ref, augd_ref, dqkv_ref)
        return 0

    lax.fori_loop(0, H // 2, pair, 0)

    def cols(j, _):
        c = pl.ds(pl.multiple_of(j * 256, 256), 256)
        d = dqkv_ref[:, c]
        dba_ref[:, c] = jnp.sum(d.astype(f32), axis=0, keepdims=True)
        dwa_ref[:, c] = dot(h_ref[...], d, TN).astype(bf)
        return 0

    lax.fori_loop(0, 3 * D // 256, cols, 0)

    def rows(i, acc):
        r = pl.ds(pl.multiple_of(i * RB, RB), RB)
        dh = dot(dqkv_ref[r, :], wa_ref[...], NT)
        n, rs = norm(x_ref[r, :].astype(f32))
        ts_ref[r, :] = (dx_ref[r, :] + norm_back(dh, n, rs, g_ref[...])).astype(bf)
        return acc[0] + jnp.sum(dh * n, axis=0, keepdims=True), acc[1] + jnp.sum(dh, axis=0, keepdims=True)

    z = jnp.zeros((1, D), f32)
    a0, a1 = lax.fori_loop(0, SEQ // RB, rows, (z, z))
    dsm_ref[0:1, :] = a0
    dsm_ref[1:2, :] = a1


def back(length, qkv, do, augq, augd, h1, x, dx, g1, wa):
    return pl.pallas_call(
        back_kernel,
        out_shape=(
            jax.ShapeDtypeStruct((SEQ, D), bf),
            jax.ShapeDtypeStruct((D, 3 * D), bf),
            jax.ShapeDtypeStruct((1, 3 * D), f32),
            jax.ShapeDtypeStruct((2, D), f32),
        ),
        in_specs=[SM] + [VM] * 9,
        out_specs=(VM,) * 4,
        scratch_shapes=[pltpu.VMEM((SEQ, 3 * D), bf), pltpu.VMEM((SEQ, D), f32)],
        compiler_params=pltpu.CompilerParams(vmem_limit_bytes=VLIMIT),
        cost_estimate=pl.CostEstimate(flops=16 * 10**9, bytes_accessed=2 * 10**7, transcendentals=12 * 2**20),
        name="back",
    )(length, qkv, do, augq, augd, h1, x, dx, g1, wa)


def shards(x, lengths, cot, g1, b1, wa, ba, wo, bo, g2, b2, w1, be, w2, br):
    def gather(v):
        return lax.all_gather(v, "shard", axis=0, tiled=True)

    smalls = [g1, b1, ba, bo, g2, b2, be, br]
    packed = lax.all_gather(jnp.concatenate(smalls), "shard", axis=0)
    full = []
    at = 0
    for v in smalls:
        full.append(packed[:, at : at + v.shape[0]].reshape(1, -1).astype(f32))
        at += v.shape[0]
    g1, b1, ba, bo, g2, b2, be, br = full
    ba = jnp.concatenate([ba[:, :D], jnp.zeros((1, D), f32), ba[:, D:]], axis=1)
    wa, wo, w1, w2 = gather(wa), gather(wo), gather(w1), gather(w2)
    h1, qkv, o, augq = front(lengths, x, g1, b1, wa, ba)
    out, dx, do, augd, dw1, dw2, dwo, dbe, sm = middle(lengths, x, o, cot, wo, bo, g2, b2, w1, be, w2, br)
    ts, dwa, dba, sm1 = back(lengths, qkv, do, augq, augd, h1, x, dx, g1, wa)

    def reduce_big(v):
        v = lax.psum_scatter(v, "shard", scatter_dimension=0, tiled=True)
        return lax.psum(v, "rep").astype(f32)

    n = lax.axis_size("shard")
    me = lax.axis_index("shard")
    parts = [sm1[0], sm1[1], dba[0, :D], dba[0, 2 * D :], sm[3], sm[1], sm[2], dbe[0], sm[0]]
    total = lax.psum(jnp.concatenate(parts), ("shard", "rep"))
    got = []
    at = 0
    for v in parts:
        got.append(total[at : at + v.shape[0]])
        at += v.shape[0]
    dg1, db1, dbq, dbv, dbo, dg2, db2, dbe, dbr = got
    dba = jnp.concatenate([dbq, dbv])

    def own(v):
        w = v.shape[0] // n
        return lax.dynamic_slice(v, (me * w,), (w,))

    return (
        out, ts, own(dg1), own(db1), reduce_big(dwa), own(dba), reduce_big(dwo), own(dbo), own(dg2), own(db2),
        reduce_big(dw1), own(dbe), reduce_big(dw2), own(dbr),
    )


def solution(mesh):
    rows = P(("shard", "rep"), None)
    vec = P("shard")
    mat = P("shard", None)
    in_specs = (rows, P(("shard", "rep")), rows, vec, vec, mat, vec, mat, vec, vec, vec, mat, vec, mat, vec)
    out_specs = (rows, rows, vec, vec, mat, vec, mat, vec, vec, vec, mat, vec, mat, vec)
    return jax.shard_map(shards, mesh=mesh, in_specs=in_specs, out_specs=out_specs, check_vma=False)
```

```python
import functools

import jax
import jax.numpy as jnp
from jax import lax
from jax.experimental import pallas as pl
from jax.experimental.pallas import tpu as pltpu
from jax.sharding import PartitionSpec as P

D = 768
H = 12
SEQ = 1024
FF = 3072
bf = jnp.bfloat16
f32 = jnp.float32
NN = (((1,), (0,)), ((), ()))
NT = (((1,), (1,)), ((), ()))
TN = (((0,), (0,)), ((), ()))
VM = pl.BlockSpec(memory_space=pltpu.VMEM)
SM = pl.BlockSpec(memory_space=pltpu.SMEM)
HB = pl.BlockSpec(memory_space=pl.ANY)
VLIMIT = 60 * 2**20
RB = 256


def dot(a, b, dims=NN):
    return lax.dot_general(a, b, dims, preferred_element_type=f32)


def lanes(shape):
    return lax.broadcasted_iota(jnp.int32, shape, 1)


def rowsi(shape):
    return lax.broadcasted_iota(jnp.int32, shape, 0)


def norm(v):
    mean = jnp.mean(v, axis=-1, keepdims=True)
    c = v - mean
    r = lax.rsqrt(jnp.mean(c * c, axis=-1, keepdims=True) + 1e-05)
    return c * r, r


def norm_back(up, n, r, gain):
    e = up * gain
    return r * (e - jnp.mean(e, axis=-1, keepdims=True) - n * jnp.mean(e * n, axis=-1, keepdims=True))


def three(v):
    hi = v.astype(bf).astype(f32)
    mid = (v - hi).astype(bf).astype(f32)
    return hi, mid, v - hi - mid


def fwd_pair(hp, length, qkv_ref, o_ref, lse_ref):
    QB = 512
    cq = pl.multiple_of(hp * 128, 128)
    q = qkv_ref[0:SEQ, pl.ds(cq, 128)]
    k = qkv_ref[SEQ : 2 * SEQ, pl.ds(cq, 128)]
    v = qkv_ref[2 * SEQ : 3 * SEQ, pl.ds(cq, 128)]
    vt = v.T
    ln = lanes((SEQ, 128))
    rw = rowsi((SEQ, 128))
    kaug = jnp.where((ln == 0) & (rw >= length), -1e30, 0.0).astype(bf)
    qaug = (lanes((QB, 128)) == 0).astype(f32).astype(bf)
    vr = rowsi((128, SEQ))
    ksides = []
    vts = []
    for h in range(2):
        half = (ln < 64) if h == 0 else (ln >= 64)
        ksides.append(jnp.concatenate([jnp.where(half, k, jnp.zeros_like(k)), kaug], axis=1))
        vh = (vr < 64) if h == 0 else (vr >= 64)
        vts.append(jnp.where(vh, vt, jnp.ones_like(vt)))
    items = [(qb, h) for qb in range(SEQ // QB) for h in range(2)]

    def scores(it):
        qb, h = it
        qs = jnp.concatenate([q[qb * QB : (qb + 1) * QB], qaug], axis=1)
        return dot(ksides[h], qs, NT)

    res = {}
    s_next = scores(items[0])
    for i, it in enumerate(items):
        s = s_next
        if i + 1 < len(items):
            s_next = scores(items[i + 1])
        m = jnp.max(s, axis=0, keepdims=True)
        p = jnp.exp(s - m).astype(bf)
        ot = dot(vts[it[1]], p)
        qb, h = it
        total = ot[64:65] if h == 0 else ot[0:1]
        res[it] = ot / total
        lse_ref[pl.ds(2 * hp + h, 1), qb * QB : (qb + 1) * QB] = m + jnp.log(total)
        if h == 1:
            op = jnp.where(rowsi((128, QB)) < 64, res[(qb, 0)], res[(qb, 1)])
            o_ref[qb * QB : (qb + 1) * QB, pl.ds(cq, 128)] = op.astype(bf).T


def bwd_pair(hp, length, qkv_ref, do_ref, augq_ref, augd_ref, dqkv_ref):
    KB = 512
    cq = pl.multiple_of(hp * 128, 128)
    q = qkv_ref[0:SEQ, pl.ds(cq, 128)]
    k = qkv_ref[SEQ : 2 * SEQ, pl.ds(cq, 128)]
    v = qkv_ref[2 * SEQ : 3 * SEQ, pl.ds(cq, 128)]
    do = do_ref[:, pl.ds(cq, 128)]
    qt = q.T
    dot_ = do.T
    qs = jnp.concatenate([q, augq_ref[...]], axis=1)
    ds_ = jnp.concatenate([do, augd_ref[...]], axis=1)
    lb = lanes((KB, 128))
    rb = rowsi((KB, 128))

    def first(it):
        kb, h = it
        half = (lb < 64) if h == 0 else (lb >= 64)
        hh = 2 * hp + h
        neg = jnp.where((lb == hh) | (lb == hh + 16) | (lb == hh + 32), -1.0, 0.0)
        aug = jnp.where((lb == 48) & (rb + kb * KB >= length), -1e30, neg).astype(bf)
        kk = k[kb * KB : (kb + 1) * KB]
        vv = v[kb * KB : (kb + 1) * KB]
        z = jnp.zeros_like(kk)
        ks = jnp.concatenate([jnp.where(half, kk, z), aug], axis=1)
        vs = jnp.concatenate([jnp.where(half, vv, z), aug], axis=1)
        return dot(qs, ks, NT), dot(ds_, vs, NT), kk

    items = [(kb, h) for kb in range(SEQ // KB) for h in range(2)]
    dq = [None, None]
    dk = {}
    dv = {}
    nxt = first(items[0])
    for i, it in enumerate(items):
        s, dp, kk = nxt
        if i + 1 < len(items):
            nxt = first(items[i + 1])
        kb, h = it
        p = jnp.exp(s)
        pb = p.astype(bf)
        dsb = (p * dp).astype(bf)
        rs = slice(0, 64) if h == 0 else slice(64, 128)
        dv[it] = dot(dot_[rs], pb)
        dk[it] = dot(qt[rs], dsb)
        t = dot(dsb, kk)
        dq[h] = t if dq[h] is None else dq[h] + t
        if h == 1:
            dkp = jnp.concatenate([dk[(kb, 0)], dk[(kb, 1)]], axis=0).astype(bf)
            dvp = jnp.concatenate([dv[(kb, 0)], dv[(kb, 1)]], axis=0).astype(bf)
            dqkv_ref[SEQ + kb * KB : SEQ + (kb + 1) * KB, pl.ds(cq, 128)] = dkp.T
            dqkv_ref[2 * SEQ + kb * KB : 2 * SEQ + (kb + 1) * KB, pl.ds(cq, 128)] = dvp.T
    dqkv_ref[0:SEQ, pl.ds(cq, 128)] = (jnp.where(lanes((SEQ, 128)) < 64, dq[0], dq[1]) * 0.125).astype(bf)


def project(h_ref, wa_ref, bias, qkv_ref):
    for i in range(3):
        t = dot(h_ref[...], wa_ref[:, i * D : (i + 1) * D])
        if bias(i) is not None:
            t = t + bias(i)
        if i == 0:
            t = t.astype(bf).astype(f32) * 0.125
        qkv_ref[i * SEQ : (i + 1) * SEQ, :] = t.astype(bf)


def front_kernel(len_ref, x_ref, g_ref, b_ref, wa_ref, ba_ref, h_ref, qkv_ref, o_ref, aug_ref, lse_ref):
    length = len_ref[0]

    def rows(i, _):
        r = pl.ds(pl.multiple_of(i * RB, RB), RB)
        n, _r = norm(x_ref[r, :].astype(f32))
        h_ref[r, :] = (n * g_ref[...] + b_ref[...]).astype(bf)
        return 0

    lax.fori_loop(0, SEQ // RB, rows, 0)

    project(h_ref, wa_ref, lambda i: ba_ref[:, i * D : (i + 1) * D], qkv_ref)
    lse_ref[...] = jnp.zeros_like(lse_ref)

    def pair(hp, _):
        fwd_pair(hp, length, qkv_ref, o_ref, lse_ref)
        return 0

    lax.fori_loop(0, H // 2, pair, 0)
    hi, mid, lo = three(lse_ref[...])
    one = jnp.where(rowsi((80, SEQ)) == 0, 1.0, 0.0)
    aug_ref[...] = jnp.concatenate([hi, mid, lo, one], axis=0).astype(bf).T


def front(length, x, g1, b1, wa, ba):
    return pl.pallas_call(
        front_kernel,
        out_shape=(
            jax.ShapeDtypeStruct((SEQ, D), bf),
            jax.ShapeDtypeStruct((3 * SEQ, D), bf),
            jax.ShapeDtypeStruct((SEQ, D), bf),
            jax.ShapeDtypeStruct((SEQ, 128), bf),
        ),
        in_specs=[SM] + [VM] * 5,
        out_specs=(VM,) * 4,
        scratch_shapes=[pltpu.VMEM((16, SEQ), f32)],
        compiler_params=pltpu.CompilerParams(vmem_limit_bytes=VLIMIT),
        cost_estimate=pl.CostEstimate(flops=7 * 10**9, bytes_accessed=10**7, transcendentals=12 * 2**20),
        name="front",
    )(length, x, g1, b1, wa, ba)


def mid_kernel(
    W, len_ref, x_ref, o_ref, cot_ref, wo_ref, bo_ref, g_ref, b_ref, w1_any, be_ref, w2_any, br_ref,
    out_ref, dx_ref, do_ref, augd_ref, dw1_ref, dw2_ref, dwo_ref, dbe_ref, dsm_ref,
    w1_ref, w2_ref, x1_ref, y_ref, dh_ref, h_ref, gb_ref, dxb_ref, sem,
):
    length = len_ref[0]
    c1 = pltpu.make_async_copy(w1_any, w1_ref, sem.at[0])
    c2 = pltpu.make_async_copy(w2_any, w2_ref, sem.at[1])
    c1.start()
    c2.start()

    def rows(i, acc):
        r = pl.ds(pl.multiple_of(i * RB, RB), RB)
        x1 = x_ref[r, :].astype(f32) + (dot(o_ref[r, :], wo_ref[...]) + bo_ref[...])
        x1_ref[r, :] = x1
        n, _r = norm(x1)
        h_ref[r, :] = (n * g_ref[...] + b_ref[...]).astype(bf)
        live = (rowsi((RB, 1)) + i * RB) < length
        gb = jnp.where(live, cot_ref[r, :].astype(f32), 0.0)
        gb_ref[r, :] = gb.astype(bf)
        y_ref[r, :] = jnp.zeros((RB, D), f32)
        dh_ref[r, :] = jnp.zeros((RB, D), f32)
        return acc + jnp.sum(gb, axis=0, keepdims=True)

    dsm_ref[0:1, :] = lax.fori_loop(0, SEQ // RB, rows, jnp.zeros((1, D), f32))
    c1.wait()
    c2.wait()

    def chunk(j, _):
        lo = pl.multiple_of(j * W, W)
        parts = [pl.ds(pl.multiple_of(lo + s * (FF // 2), W), W) for s in range(2)]
        for s, c in enumerate(parts):
            w1 = w1_ref[:, c]
            w2 = w2_ref[c, :]
            u = dot(h_ref[...], w1) + be_ref[:, c]
            sig = 0.5 * jnp.tanh(0.851 * u) + 0.5
            a = u * sig
            ab = a.astype(bf)
            y_ref[...] += dot(ab, w2)
            dw2_ref[c, :] = dot(ab, gb_ref[...], TN).astype(bf)
            da = dot(gb_ref[...], w2, NT)
            du = da * (sig * (1.0 + 1.702 * (u - a)))
            dub = du.astype(bf)
            dbe_ref[:, c] = jnp.sum(du, axis=0, keepdims=True)
            dw1_ref[:, c] = dot(h_ref[...], dub, TN).astype(bf)
            dh_ref[...] += dot(dub, w1, NT)
        return 0

    lax.fori_loop(0, FF // (2 * W), chunk, 0)
    hl = lanes((D, 128)) % 16
    sel = jnp.where((hl == rowsi((D, 128)) // 64) & (lanes((D, 128)) < 48), 1.0, 0.0).astype(bf)

    def last(i, acc):
        r = pl.ds(pl.multiple_of(i * RB, RB), RB)
        x1 = x1_ref[r, :]
        live = (rowsi((RB, 1)) + i * RB) < length
        out_ref[r, :] = jnp.where(live, x1 + (y_ref[r, :] + br_ref[...]), 0.0).astype(bf)
        n, rs = norm(x1)
        dh = dh_ref[r, :]
        dx = gb_ref[r, :].astype(f32) + norm_back(dh, n, rs, g_ref[...])
        dx_ref[r, :] = dx
        dxb = dx.astype(bf)
        dxb_ref[r, :] = dxb
        do = dot(dxb, wo_ref[...], NT).astype(bf)
        do_ref[r, :] = do
        prod = do.astype(f32) * o_ref[r, :].astype(f32)
        phi = prod.astype(bf)
        dl = dot(phi, sel) + dot((prod - phi.astype(f32)).astype(bf), sel)
        hi, mid, lo = three(dl)
        ln = lanes((RB, 128))
        augd_ref[r, :] = jnp.where(ln < 16, hi, jnp.where(ln < 32, mid, lo)).astype(bf)
        return (
            acc[0] + jnp.sum(dh * n, axis=0, keepdims=True),
            acc[1] + jnp.sum(dh, axis=0, keepdims=True),
            acc[2] + jnp.sum(dx, axis=0, keepdims=True),
        )

    z = jnp.zeros((1, D), f32)
    a0, a1, a2 = lax.fori_loop(0, SEQ // RB, last, (z, z, z))
    dsm_ref[1:2, :] = a0
    dsm_ref[2:3, :] = a1
    dsm_ref[3:4, :] = a2
    dwo_ref[...] = dot(o_ref[...], dxb_ref[...], TN).astype(bf)


def middle(length, x, o, cot, wo, bo, g2, b2, w1, be, w2, br):
    return pl.pallas_call(
        functools.partial(mid_kernel, 256),
        out_shape=(
            jax.ShapeDtypeStruct((SEQ, D), bf),
            jax.ShapeDtypeStruct((SEQ, D), f32),
            jax.ShapeDtypeStruct((SEQ, D), bf),
            jax.ShapeDtypeStruct((SEQ, 128), bf),
            jax.ShapeDtypeStruct((D, FF), bf),
            jax.ShapeDtypeStruct((FF, D), bf),
            jax.ShapeDtypeStruct((D, D), bf),
            jax.ShapeDtypeStruct((1, FF), f32),
            jax.ShapeDtypeStruct((4, D), f32),
        ),
        in_specs=[SM] + [VM] * 7 + [HB, VM, HB, VM],
        out_specs=(VM,) * 9,
        scratch_shapes=[
            pltpu.VMEM((D, FF), bf),
            pltpu.VMEM((FF, D), bf),
            pltpu.VMEM((SEQ, D), f32),
            pltpu.VMEM((SEQ, D), f32),
            pltpu.VMEM((SEQ, D), f32),
            pltpu.VMEM((SEQ, D), bf),
            pltpu.VMEM((SEQ, D), bf),
            pltpu.VMEM((SEQ, D), bf),
            pltpu.SemaphoreType.DMA((2,)),
        ],
        compiler_params=pltpu.CompilerParams(vmem_limit_bytes=VLIMIT),
        cost_estimate=pl.CostEstimate(flops=33 * 10**9, bytes_accessed=3 * 10**7, transcendentals=3 * 2**20),
        name="middle",
    )(length, x, o, cot, wo, bo, g2, b2, w1, be, w2, br)


def back_kernel(len_ref, qkv_ref, do_ref, augq_ref, augd_ref, h_ref, x_ref, dx_ref, g_ref, wa_ref,
                ts_ref, dwa_ref, dba_ref, dsm_ref, dqkv_ref):
    length = len_ref[0]

    def pair(hp, _):
        bwd_pair(hp, length, qkv_ref, do_ref, augq_ref, augd_ref, dqkv_ref)
        return 0

    lax.fori_loop(0, H // 2, pair, 0)

    for i in range(3):
        d = dqkv_ref[i * SEQ : (i + 1) * SEQ, :]
        dba_ref[:, i * D : (i + 1) * D] = jnp.sum(d.astype(f32), axis=0, keepdims=True)
        dwa_ref[:, i * D : (i + 1) * D] = dot(h_ref[...], d, TN).astype(bf)

    def rows(i, acc):
        r = pl.ds(pl.multiple_of(i * RB, RB), RB)
        dh = jnp.zeros((RB, D), f32)
        for k in range(3):
            d = dqkv_ref[pl.ds(pl.multiple_of(i * RB + k * SEQ, RB), RB), :]
            dh = dh + dot(d, wa_ref[:, k * D : (k + 1) * D], NT)
        n, rs = norm(x_ref[r, :].astype(f32))
        ts_ref[r, :] = (dx_ref[r, :] + norm_back(dh, n, rs, g_ref[...])).astype(bf)
        return acc[0] + jnp.sum(dh * n, axis=0, keepdims=True), acc[1] + jnp.sum(dh, axis=0, keepdims=True)

    z = jnp.zeros((1, D), f32)
    a0, a1 = lax.fori_loop(0, SEQ // RB, rows, (z, z))
    dsm_ref[0:1, :] = a0
    dsm_ref[1:2, :] = a1


def back(length, qkv, do, augq, augd, h1, x, dx, g1, wa):
    return pl.pallas_call(
        back_kernel,
        out_shape=(
            jax.ShapeDtypeStruct((SEQ, D), bf),
            jax.ShapeDtypeStruct((D, 3 * D), bf),
            jax.ShapeDtypeStruct((1, 3 * D), f32),
            jax.ShapeDtypeStruct((2, D), f32),
        ),
        in_specs=[SM] + [VM] * 9,
        out_specs=(VM,) * 4,
        scratch_shapes=[pltpu.VMEM((3 * SEQ, D), bf)],
        compiler_params=pltpu.CompilerParams(vmem_limit_bytes=VLIMIT),
        cost_estimate=pl.CostEstimate(flops=16 * 10**9, bytes_accessed=2 * 10**7, transcendentals=12 * 2**20),
        name="back",
    )(length, qkv, do, augq, augd, h1, x, dx, g1, wa)


def plain_shards(x, lengths, cot, g1, b1, wa, ba, wo, bo, g2, b2, w1, be, w2, br):
    def gather(v):
        return lax.all_gather(v, "shard", axis=0, tiled=True)

    smalls = [g1, b1, ba, bo, g2, b2, be, br]
    packed = lax.all_gather(jnp.concatenate(smalls), "shard", axis=0)
    full = []
    at = 0
    for v in smalls:
        full.append(packed[:, at : at + v.shape[0]].reshape(1, -1).astype(f32))
        at += v.shape[0]
    g1, b1, ba, bo, g2, b2, be, br = full
    ba = jnp.concatenate([ba[:, :D], jnp.zeros((1, D), f32), ba[:, D:]], axis=1)
    wa, wo, w1, w2 = gather(wa), gather(wo), gather(w1), gather(w2)
    h1, qkv, o, augq = front(lengths, x, g1, b1, wa, ba)
    out, dx, do, augd, dw1, dw2, dwo, dbe, sm = middle(lengths, x, o, cot, wo, bo, g2, b2, w1, be, w2, br)
    ts, dwa, dba, sm1 = back(lengths, qkv, do, augq, augd, h1, x, dx, g1, wa)

    def reduce_big(v):
        v = lax.psum_scatter(v, "shard", scatter_dimension=0, tiled=True)
        return lax.psum(v, "rep").astype(f32)

    n = lax.axis_size("shard")
    me = lax.axis_index("shard")
    parts = [sm1[0], sm1[1], dba[0, :D], dba[0, 2 * D :], sm[3], sm[1], sm[2], dbe[0], sm[0]]
    total = lax.psum(jnp.concatenate(parts), ("shard", "rep"))
    got = []
    at = 0
    for v in parts:
        got.append(total[at : at + v.shape[0]])
        at += v.shape[0]
    dg1, db1, dbq, dbv, dbo, dg2, db2, dbe, dbr = got
    dba = jnp.concatenate([dbq, dbv])

    def own(v):
        w = v.shape[0] // n
        return lax.dynamic_slice(v, (me * w,), (w,))

    return (
        out, ts, own(dg1), own(db1), reduce_big(dwa), own(dba), reduce_big(dwo), own(dbo), own(dg2), own(db2),
        reduce_big(dw1), own(dbe), reduce_big(dw2), own(dbr),
    )


MESH = pl.DeviceIdType.MESH
HF = D // 2
NCHUNK = 12
G1, B1, BA, BO, G2, B2, BE, BR = 0, 1, 2, 4, 5, 6, 7, 11


class Place:
    def __init__(self):
        s = lax.axis_index("shard")
        r = lax.axis_index("rep")
        core = r % 2
        x = (r // 2) % 2
        z = r // 4
        self.s, self.core, self.x, self.a, self.b = s, core, x, (z % 2 + z // 2) % 2, z // 2
        self.to = {
            "core": (s, r + 1 - 2 * core),
            "y": (1 - s, r),
            "x": (s, r + 2 - 4 * x),
            "a": (s, r + 4 - 8 * (z % 2)),
            "b": (s, r + 4 * (3 - 2 * z)),
        }

    def greet(self):
        barrier = pltpu.get_barrier_semaphore()
        for d in self.to.values():
            pl.semaphore_signal(barrier, inc=1, device_id=d, device_id_type=MESH)
        pl.semaphore_wait(barrier, len(self.to))


def remote(src, dst, send, recv, to):
    return pltpu.make_async_remote_copy(
        src_ref=src, dst_ref=dst, send_sem=send, recv_sem=recv, device_id=to, device_id_type=MESH
    )


class Unit:
    def __init__(self, place, index, own, full, r0, nr, c0, width, send, recv):
        self.p, self.i, self.own, self.full = place, index, own, full
        self.r0, self.n, self.half = r0, nr // 8, own.shape[0]
        w = width // 2
        self.cols = [pl.ds(c0, w), pl.ds(c0 + w, w)]
        self.send, self.recv = send, recv

    def copies(self, step):
        p, n = self.p, self.n
        out = []
        for k, zc in enumerate((p.a, p.b)):
            spot = p.core * 4 + zc * 2 + p.x
            other = (1 - p.s) * self.half + self.r0
            sems = (self.send.at[self.i, step, k], self.recv.at[self.i, step, k])
            if step == 0:
                src = self.own.at[pl.ds(pl.multiple_of(self.r0 + spot * n, 16), n), self.cols[k]]
                dst = self.full.at[pl.ds(pl.multiple_of(p.s * self.half + self.r0 + spot * n, 16), n), self.cols[k]]
                out.append(remote(src, dst, *sems, p.to["y"]))
                continue
            if step == 1:
                at, m, to = spot, 1, p.to["x"]
            elif step == 2:
                at, m, to = p.core * 4 + zc * 2, 2, p.to["ab"[k]]
            else:
                at, m, to = p.core * 4, 4, p.to["core"]
            ref = self.full.at[pl.ds(pl.multiple_of(other + at * n, 16), m * n), self.cols[k]]
            out.append(remote(ref, ref, *sems, to))
        return out

    def start(self, step):
        for c in self.copies(step):
            c.start()

    def wait(self, step):
        for c in self.copies(step):
            c.wait()

    def move(self, step):
        self.wait(step - 1)
        if step < 4:
            self.start(step)


def vec(sm_ref, row, rows=1):
    return jnp.concatenate([sm_ref[0, row : row + rows], sm_ref[1, row : row + rows]], axis=1)


def lead_kernel(
    len_ref, x_ref, sm_own, wa_own, wo_own, w1_own, w2_own,
    h_ref, qkv_ref, o_ref, aug_ref, wa_ref, sm_ref, wo_ref, w1_ref, w2_ref,
    lse_ref, send, recv, sm_send, sm_recv, lsem,
):
    place = Place()
    length = len_ref[0]
    s = place.s
    local = []
    for i, (own, full) in enumerate(((wa_own, wa_ref), (wo_own, wo_ref), (w1_own, w1_ref), (w2_own, w2_ref))):
        m = own.shape[0]
        local.append(pltpu.make_async_copy(own, full.at[pl.ds(pl.multiple_of(s * m, 16), m)], lsem.at[i]))
    local.append(pltpu.make_async_copy(sm_own, sm_ref.at[s], lsem.at[4]))
    for c in local:
        c.start()
    specs = [(wa_own, wa_ref, 0, HF, i * D, D) for i in range(3)]
    specs += [(wo_own, wo_ref, 0, HF, 0, D), (w1_own, w1_ref, 0, HF, 0, 2 * D)]
    specs += [(w1_own, w1_ref, 0, HF, 2 * D, 2 * D), (w2_own, w2_ref, 0, D, 0, D)]
    specs += [(w2_own, w2_ref, D, D, 0, D)]
    units = [Unit(place, i, *t, send, recv) for i, t in enumerate(specs)]
    groups = [units[3:5], units[5:7], units[7:8]]
    place.greet()
    smc = remote(sm_own, sm_ref.at[s], sm_send, sm_recv, place.to["y"])
    smc.start()
    for u in units[:3]:
        u.start(0)
    local[4].wait()
    smc.wait()
    g1, b1 = vec(sm_ref, G1), vec(sm_ref, B1)

    def rows(i, _):
        r = pl.ds(pl.multiple_of(i * RB, RB), RB)
        n, _r = norm(x_ref[r, :].astype(f32))
        h_ref[r, :] = (n * g1 + b1).astype(bf)
        return 0

    lax.fori_loop(0, SEQ // RB, rows, 0)
    for u in units[:3]:
        u.move(1)
    for u in units[3:]:
        u.start(0)
    for u in units[:3]:
        u.move(2)
    for u in units[:3]:
        u.move(3)
    for u in units[:3]:
        u.move(4)
    local[0].wait()
    bias = [
        jnp.concatenate([sm_ref[0, BA : BA + 1], sm_ref[0, BA + 1 : BA + 2]], axis=1),
        None,
        jnp.concatenate([sm_ref[1, BA : BA + 1], sm_ref[1, BA + 1 : BA + 2]], axis=1),
    ]
    project(h_ref, wa_ref, lambda i: bias[i], qkv_ref)
    lse_ref[...] = jnp.zeros_like(lse_ref)

    def go(group, step):
        for u in groups[group]:
            u.move(step)

    go(0, 1)

    def pair(hp, _):
        fwd_pair(hp, length, qkv_ref, o_ref, lse_ref)
        for t in range(5):

            @pl.when(hp == t)
            def _(t=t):
                for group in range(3):
                    step = t + 2 - group
                    if 1 <= step <= 4:
                        go(group, step)

        return 0

    lax.fori_loop(0, H // 2, pair, 0)
    hi, mid, lo = three(lse_ref[...])
    one = jnp.where(rowsi((80, SEQ)) == 0, 1.0, 0.0)
    aug_ref[...] = jnp.concatenate([hi, mid, lo, one], axis=0).astype(bf).T
    for c in local[1:4]:
        c.wait()


def lead(length, x, sm, wa, wo, w1, w2):
    sds = jax.ShapeDtypeStruct
    return pl.pallas_call(
        lead_kernel,
        out_shape=(
            sds((SEQ, D), bf),
            sds((3 * SEQ, D), bf),
            sds((SEQ, D), bf),
            sds((SEQ, 128), bf),
            sds((D, 3 * D), bf),
            sds((2, 16, HF), f32),
            sds((D, D), bf),
            sds((D, FF), bf),
            sds((FF, D), bf),
        ),
        in_specs=[SM, VM, VM] + [HB] * 4,
        out_specs=(VM,) * 6 + (HB,) * 3,
        scratch_shapes=[
            pltpu.VMEM((16, SEQ), f32),
            pltpu.SemaphoreType.DMA((8, 4, 2)),
            pltpu.SemaphoreType.DMA((8, 4, 2)),
            pltpu.SemaphoreType.DMA(()),
            pltpu.SemaphoreType.DMA(()),
            pltpu.SemaphoreType.DMA((5,)),
        ],
        compiler_params=pltpu.CompilerParams(vmem_limit_bytes=VLIMIT, collective_id=0, has_side_effects=True),
        cost_estimate=pl.CostEstimate(flops=7 * 10**9, bytes_accessed=10**7, transcendentals=12 * 2**20),
        name="lead",
    )(length, x, sm, wa, wo, w1, w2)


class Reduce:
    STEPS = ("core", "y", "x", "a", "b", "b", "a", "x", "core")

    def __init__(self, place, first, sums, lands, total, send, recv, keep_sem):
        self.p, self.f, self.k, self.l, self.g = place, first, sums, lands, total
        self.send, self.recv, self.keep_sem = send, recv, keep_sem

    def rows(self, at, n):
        return pl.ds(pl.multiple_of(at, 16), n)

    def copy(self, step, c):
        p, slot, two = self.p, c % 4, c % 2
        sems = (self.send.at[step, slot], self.recv.at[step, slot], p.to[self.STEPS[step]])
        if step == 0:
            return remote(self.f.at[two, 1 - p.core], self.l[0].at[slot], *sems)
        if step < 5:
            n = D >> step
            away = 1 - (p.s, p.x, p.a, p.b)[step - 1]
            return remote(self.k[step - 1].at[two, self.rows(away * n, n)], self.l[step].at[slot], *sems)
        base = p.core * HF
        if step == 5:
            at = base + (p.x * 4 + p.a * 2 + p.b) * 48
            return remote(self.k[4].at[two], self.g.at[c, self.rows(at, 48)], *sems)
        if step == 6:
            at, n = base + (p.x * 4 + p.a * 2) * 48, 96
        elif step == 7:
            at, n = base + p.x * 192, 192
        else:
            at, n = base, HF
        ref = self.g.at[c, self.rows(at, n)]
        return remote(ref, ref, *sems)

    def keep(self, c):
        p = self.p
        at = p.core * HF + (p.x * 4 + p.a * 2 + p.b) * 48
        return pltpu.make_async_copy(self.k[4].at[c % 2], self.g.at[c, self.rows(at, 48)], self.keep_sem.at[c % 2])

    def stage(self, step, c):
        p, slot, two = self.p, c % 4, c % 2
        if step > 0:
            self.copy(step - 1, c).wait()
        if 1 <= step <= 5:
            n = D >> (step - 1)
            if step == 1:
                mine = self.f[two, p.core]
            else:
                bit = (p.s, p.x, p.a, p.b)[step - 2]
                mine = self.k[step - 2][two, self.rows(bit * n, n)]
            self.k[step - 1][two] = (mine.astype(f32) + self.l[step - 1][slot].astype(f32)).astype(bf)
        if step == 5:
            self.keep(c).start()
        if step == 6:
            self.keep(c).wait()
        if step < 9:
            self.copy(step, c).start()

    def tick(self, t):
        for step in range(9, -1, -1):
            e = t - step
            if isinstance(e, int):
                if 0 <= e <= 14 and (e <= 8 or e % 2 == 0):
                    self.stage(step, e if e <= 8 else 4 + e // 2)
                continue

            @pl.when((e >= 0) & (e <= 14) & ((e <= 8) | (e % 2 == 0)))
            def _(step=step, e=e):
                self.stage(step, jnp.where(e <= 8, e, 4 + e // 2))


def rest_kernel(
    len_ref, sm_ref, x_any, o_any, cot_any, h1_any, qkv_any, augq_ref, wo_any, wa_any, w1_any, w2_any,
    out_any, ts_any, g_any, sv_ref,
    m1, m2, wo, wa, t1, t2, o_ref, gb_ref, h_ref, dxb_ref, do_ref, augd_ref, x1_ref, y_ref, dh_ref,
    first, k0, k1, k2, k3, k4, l0, l1, l2, l3, l4, sva, svl,
    lsem, osem, send, recv, keep_sem, svs, svr,
):
    place = Place()
    red = Reduce(place, first, (k0, k1, k2, k3, k4), (l0, l1, l2, l3, l4), g_any, send, recv, keep_sem)
    length = len_ref[0]

    def load(i, src, dst):
        c = pltpu.make_async_copy(src, dst, lsem.at[i])
        c.start()
        return c

    early = [load(0, x_any, t1), load(1, o_any, o_ref), load(2, cot_any, gb_ref), load(3, wo_any, wo)]
    weights = []
    for j in range(4):
        for h in range(2):
            away = pl.ds(j * D + h * HF, HF)
            near = pl.ds(h * (FF // 2) + j * HF, HF)
            weights.append(load(4 + 4 * j + 2 * h, w1_any.at[:, near], m1.at[pl.ds(j * D, D), pl.ds(h * HF, HF)]))
            weights.append(load(5 + 4 * j + 2 * h, w2_any.at[near, :], m2.at[away, :]))
    place.greet()
    wal = load(20, wa_any, wa)
    for c in early:
        c.wait()
    bo, g2, b2, br = vec(sm_ref, BO), vec(sm_ref, G2), vec(sm_ref, B2), vec(sm_ref, BR)

    def rows1(i, acc):
        r = pl.ds(pl.multiple_of(i * RB, RB), RB)
        x1 = t1[r, :].astype(f32) + (dot(o_ref[r, :], wo[...]) + bo)
        x1_ref[r, :] = x1
        y_ref[r, :] = x1 + br
        n, _r = norm(x1)
        h_ref[r, :] = (n * g2 + b2).astype(bf)
        live = (rowsi((RB, 1)) + i * RB) < length
        gb = jnp.where(live, gb_ref[r, :].astype(f32), 0.0)
        gb_ref[r, :] = gb.astype(bf)
        dh_ref[r, :] = jnp.zeros((RB, D), f32)
        return acc + jnp.sum(gb, axis=0, keepdims=True)

    sva[0, 12:16, :] = jnp.zeros((4, D), f32)
    sva[0, 7:8, :] = lax.fori_loop(0, SEQ // RB, rows1, jnp.zeros((1, D), f32))
    for c in weights:
        c.wait()

    def emit(c, value):
        for h in range(2):
            first[c % 2, h] = value[:, h * HF : (h + 1) * HF].astype(bf)

    def hidden(j, _):
        rj = pl.ds(pl.multiple_of(j * D, D), D)
        be = jnp.concatenate([sm_ref[0, pl.ds(BE + j, 1), :], sm_ref[1, pl.ds(BE + j, 1), :]], axis=1)
        NB = 512

        def rows2(i, acc):
            r = pl.ds(pl.multiple_of(i * NB, NB), NB)
            u = dot(h_ref[r, :], m1[rj, :]) + be
            sig = 0.5 * jnp.tanh(0.851 * u) + 0.5
            a = u * sig
            ab = a.astype(bf)
            t1[r, :] = ab
            y_ref[r, :] += dot(ab, m2[rj, :])
            da = dot(gb_ref[r, :], m2[rj, :], NT)
            du = da * (sig * (1.0 + 1.702 * (u - a)))
            dub = du.astype(bf)
            t2[r, :] = dub
            dh_ref[r, :] += dot(dub, m1[rj, :], NT)
            return acc + jnp.sum(du, axis=0, keepdims=True)

        sva[0, pl.ds(8 + j, 1), :] = lax.fori_loop(0, SEQ // NB, rows2, jnp.zeros((1, D), f32))
        emit(0, dot(t1[...], gb_ref[...], TN))
        red.tick(2 * j)
        emit(1, dot(h_ref[...], t2[...], TN))
        red.tick(2 * j + 1)
        return 0

    lax.fori_loop(0, 4, hidden, 0)
    late = [load(0, qkv_any, m1), load(1, h1_any, h_ref), load(2, x_any, t2)]
    ln = lanes((RB, 128))
    sel = ((lanes((D, 128)) % 16 == rowsi((D, 128)) // 64) & (lanes((D, 128)) < 48)).astype(f32).astype(bf)

    def rows3(i, acc):
        r = pl.ds(pl.multiple_of(i * RB, RB), RB)
        x1 = x1_ref[r, :]
        live = (rowsi((RB, 1)) + i * RB) < length
        t1[r, :] = jnp.where(live, y_ref[r, :], 0.0).astype(bf)
        n, rs = norm(x1)
        dh = dh_ref[r, :]
        dx = gb_ref[r, :].astype(f32) + norm_back(dh, n, rs, g2)
        x1_ref[r, :] = dx
        dxb = dx.astype(bf)
        dxb_ref[r, :] = dxb
        do = dot(dxb, wo[...], NT).astype(bf)
        do_ref[r, :] = do
        prod = do.astype(f32) * o_ref[r, :].astype(f32)
        phi = prod.astype(bf)
        dl = dot(phi, sel) + dot((prod - phi.astype(f32)).astype(bf), sel)
        hi, mid, lo = three(dl)
        augd_ref[r, :] = jnp.where(ln < 16, hi, jnp.where(ln < 32, mid, lo)).astype(bf)
        return (
            acc[0] + jnp.sum(dh * n, axis=0, keepdims=True),
            acc[1] + jnp.sum(dh, axis=0, keepdims=True),
            acc[2] + jnp.sum(dx, axis=0, keepdims=True),
        )

    z = jnp.zeros((1, D), f32)
    a0, a1, a2 = lax.fori_loop(0, SEQ // RB, rows3, (z, z, z))
    sva[0, 5:6, :] = a0
    sva[0, 6:7, :] = a1
    sva[0, 4:5, :] = a2
    out_copy = pltpu.make_async_copy(t1, out_any, osem.at[0])
    out_copy.start()
    emit(0, dot(o_ref[...], dxb_ref[...], TN))
    red.tick(8)
    for c in late:
        c.wait()

    def pair(hp, _):
        bwd_pair(hp, length, m1, do_ref, augq_ref, augd_ref, m2)

        @pl.when(hp % 2 == 1)
        def _():
            c = pl.ds(pl.multiple_of((hp // 2) * 256, 256), 256)
            parts = [dot(h_ref[...], m2[k * SEQ : (k + 1) * SEQ, c], TN).astype(bf) for k in range(3)]
            two = (9 + hp // 2) % 2
            first[two, 0, :, 0:256] = parts[0]
            first[two, 0, :, 256:384] = parts[1][:, 0:128]
            first[two, 1, :, 0:128] = parts[1][:, 128:256]
            first[two, 1, :, 128:384] = parts[2]

        red.tick(9 + hp)
        return 0

    lax.fori_loop(0, H // 2, pair, 0)
    for k, row in ((0, 2), (2, 3)):
        sva[0, row : row + 1, :] = jnp.sum(m2[k * SEQ : (k + 1) * SEQ, :].astype(f32), axis=0, keepdims=True)
    wal.wait()
    g1 = vec(sm_ref, G1)

    def rows4(i, acc):
        r = pl.ds(pl.multiple_of(i * RB, RB), RB)
        dh = jnp.zeros((RB, D), f32)
        for k in range(3):
            d = m2[pl.ds(pl.multiple_of(i * RB + k * SEQ, RB), RB), :]
            dh = dh + dot(d, wa[:, k * D : (k + 1) * D], NT)
        n, rs = norm(t2[r, :].astype(f32))
        gb_ref[r, :] = (x1_ref[r, :] + norm_back(dh, n, rs, g1)).astype(bf)
        red.tick(15 + i)
        return acc[0] + jnp.sum(dh * n, axis=0, keepdims=True), acc[1] + jnp.sum(dh, axis=0, keepdims=True)

    a0, a1 = lax.fori_loop(0, SEQ // RB, rows4, (z, z))
    sva[0, 0:1, :] = a0
    sva[0, 1:2, :] = a1
    ts_copy = pltpu.make_async_copy(gb_ref, ts_any, osem.at[1])
    ts_copy.start()

    def sv(step):
        return remote(sva.at[step], svl.at[step], svs.at[step], svr.at[step], place.to[red.STEPS[step]])

    sv(0).start()
    for step in range(5):
        red.tick(19 + step)
        sv(step).wait()
        total = sva[step] + svl[step]
        if step < 4:
            sva[step + 1] = total
            sv(step + 1).start()
        else:
            sv_ref[...] = total
    out_copy.wait()
    ts_copy.wait()


def rest(length, sm, x, o, cot, h1, qkv, augq, wo, wa, w1, w2):
    sds = jax.ShapeDtypeStruct
    V = pltpu.VMEM
    dma = pltpu.SemaphoreType.DMA
    return pl.pallas_call(
        rest_kernel,
        out_shape=(
            sds((SEQ, D), bf),
            sds((SEQ, D), bf),
            sds((NCHUNK, D, HF), bf),
            sds((16, D), f32),
        ),
        in_specs=[SM, VM] + [HB] * 5 + [VM] + [HB] * 4,
        out_specs=(HB, HB, HB, VM),
        scratch_shapes=[
            V((FF, D), bf), V((FF, D), bf), V((D, D), bf), V((D, 3 * D), bf),
            V((SEQ, D), bf), V((SEQ, D), bf), V((SEQ, D), bf), V((SEQ, D), bf), V((SEQ, D), bf),
            V((SEQ, D), bf), V((SEQ, D), bf), V((SEQ, 128), bf),
            V((SEQ, D), f32), V((SEQ, D), f32), V((SEQ, D), f32),
            V((2, 2, D, HF), bf),
            V((2, D, HF), bf), V((2, 384, HF), bf), V((2, 192, HF), bf), V((2, 96, HF), bf), V((2, 48, HF), bf),
            V((4, D, HF), bf), V((4, 384, HF), bf), V((4, 192, HF), bf), V((4, 96, HF), bf), V((4, 48, HF), bf),
            V((5, 16, D), f32), V((5, 16, D), f32),
            dma((21,)), dma((2,)), dma((9, 4)), dma((9, 4)), dma((2,)), dma((5,)), dma((5,)),
        ],
        compiler_params=pltpu.CompilerParams(vmem_limit_bytes=VLIMIT, collective_id=1, has_side_effects=True),
        cost_estimate=pl.CostEstimate(flops=49 * 10**9, bytes_accessed=5 * 10**7, transcendentals=15 * 2**20),
        name="rest",
    )(length, sm, x, o, cot, h1, qkv, augq, wo, wa, w1, w2)


def shards(x, lengths, cot, g1, b1, wa, ba, wo, bo, g2, b2, w1, be, w2, br):
    sm = jnp.concatenate([g1, b1, ba, bo, g2, b2, be, br]).astype(f32).reshape(12, HF)
    sm = jnp.pad(sm, ((0, 4), (0, 0)))
    h1, qkv, o, augq, wa, sm, wo, w1, w2 = lead(lengths, x, sm, wa, wo, w1, w2)
    out, ts, g, sv = rest(lengths, sm, x, o, cot, h1, qkv, augq, wo, wa, w1, w2)
    me = lax.axis_index("shard")
    g = g.reshape(NCHUNK, 2, HF, HF)
    dw2 = g[0:8:2].transpose(0, 2, 1, 3).reshape(FF // 2, D).astype(f32)
    dw1 = g[1:8:2].transpose(2, 1, 0, 3).reshape(HF, FF).astype(f32)
    dwo = g[8].transpose(1, 0, 2).reshape(HF, D).astype(f32)
    dwa = g[9:].transpose(0, 2, 1, 3).reshape(3, HF, 3, 256).transpose(1, 2, 0, 3).reshape(HF, 3 * D).astype(f32)
    half = lax.dynamic_slice(sv, (0, me * HF), (16, HF))
    dba = lax.dynamic_slice(sv[2:4], (me, 0), (1, D))[0]
    return (
        out, ts, half[0], half[1], dwa, dba, dwo, half[4], half[5], half[6], dw1, half[8:12].reshape(-1), dw2, half[7],
    )


def solution(mesh):
    rows = P(("shard", "rep"), None)
    vec = P("shard")
    mat = P("shard", None)
    in_specs = (rows, P(("shard", "rep")), rows, vec, vec, mat, vec, mat, vec, vec, vec, mat, vec, mat, vec)
    out_specs = (rows, rows, vec, vec, mat, vec, mat, vec, vec, vec, mat, vec, mat, vec)
    body = shards if mesh.shape["shard"] == 2 and mesh.shape["rep"] == 16 else plain_shards
    return jax.shard_map(body, mesh=mesh, in_specs=in_specs, out_specs=out_specs, check_vma=False)
```
